128 devices in a mesh: row: 4 (over y_lo, core), col: 32 (over y_hi, x, z).
Axes of the slice: x: 4, y: 4 (y_hi: 2, y_lo: 2; y = y_hi * 2 + y_lo), z: 4, core: 2. Of those that a mesh axis runs over, the one named last changes fastest.
Arguments:
- slab: bfloat16 [4096, 8192], P('row', 'col'), may hold values from -6 to 6
- slab_mask: int32 [16, 32], P('row', 'col'), may hold values from 0 to 1, as said below
- order: int32 [32], replicated, may hold values from 0 to 31, each once
- integrals: bfloat16 [2, 16384, 32768], P(None, 'row', 'col'), may hold values from -0.0625 to 0.0625
- integral_mask: int32 [2, 64, 128], P(None, 'row', 'col'), may hold values 0 or 1
- row_owner: int32 [2], replicated, may hold values from 0 to 3
Outputs:
- ladder: bfloat16 [4096, 32768], P('row', 'col')
The draws below stay inside these ranges and needn't reach their ends.
Inputs may be any that keep to these rules, and one draw needn't show every extreme that they name: `slab_mask`: each block of 4 row tiles by 1 arrival tiles that one device holds has exactly 3 nonzero tiles; rows of tiles differ in their share. `order`: each of 0 to 31 once.
All inputs are finite; a program needn't handle non-finite values. No bound on the sum of `integral_mask` on one device may be relied on, other than what follows from the above.
Results may differ from the reference program's by a relative error of at most 0.001.
Values may be sent and summed in bfloat16 or wider, within the bound.
No kernel may reach another device: no remote copies, remote signals or barrier semaphores. Data moves between devices by JAX's collectives and lax.ppermute only.
A program may use at most 192 MiB of HBM per device.

```python
import jax
import jax.numpy as jnp
from jax import lax

TW = 256
PT = 16
STEPS = 2
LOCAL_ROW_TILES = 4
ROW_TILE_COUNT = 16
CONTRACT_TILES = 32
KEY_COL_TILES = 1
CAP = 3
KP = 4096
M = 4096
K = 8192
NTILES = 128
N = 32768
N_ROW = 4
N_COL = 32


def draw_slab_mask(key, part):
    key = jax.random.fold_in(key, 11)
    first_operand, second_operand = jax.random.split(key)
    tile_blocks = ROW_TILE_COUNT // LOCAL_ROW_TILES
    count = LOCAL_ROW_TILES * KEY_COL_TILES
    sparsity_level = jax.random.randint(first_operand, (ROW_TILE_COUNT, 1), 1, 9)
    random_noise = jax.random.randint(second_operand, (ROW_TILE_COUNT, CONTRACT_TILES), 0, 12)
    scores = sparsity_level * 12 + random_noise
    scores = scores.reshape(tile_blocks, LOCAL_ROW_TILES, N_COL, KEY_COL_TILES).transpose(0, 2, 1, 3).reshape(tile_blocks, N_COL, count)
    scores = scores * count + jnp.arange(count, dtype=jnp.int32)
    values, chosen = jax.lax.top_k(scores, CAP)
    places = jnp.arange(count, dtype=jnp.int32)
    picked_tiles = jnp.any(places[None, None, None, :] == chosen[..., None], axis=2).astype(jnp.int32)
    return picked_tiles.reshape(tile_blocks, N_COL, LOCAL_ROW_TILES, KEY_COL_TILES).transpose(0, 2, 1, 3).reshape(ROW_TILE_COUNT, CONTRACT_TILES)


def set_ends(result, stream_key, least, high):
    spot = [jax.random.randint(jax.random.fold_in(stream_key, axis), (), 0, length) for axis, length in enumerate(result.shape)]
    widest = result.shape.index(max(result.shape))
    beside = spot[:widest] + [(spot[widest] + 1) % result.shape[widest]] + spot[widest + 1:]
    return result.at[tuple(spot)].set(least).at[tuple(beside)].set(high)


def block_scale(own_key, extent, pieces, low, top_value):
    loudness = 1.0
    for position, parts in pieces:
        draws = jax.random.uniform(jax.random.fold_in(jax.random.fold_in(own_key, 6), position), (parts,), jnp.float32, low / len(pieces), top_value / len(pieces))
        loudness = loudness * jnp.repeat(jnp.exp(draws), extent[position] // parts).reshape((-1,) + (1,) * (len(extent) - 1 - position))
    return loudness


def scatter_about(rng, dims, scale, limit, cuts=(), kind=jnp.bfloat16):
    values = scale * jax.random.normal(rng, dims, jnp.float32)
    if cuts:
        values = values * block_scale(rng, dims, cuts, -0.22, 0.18)
    return jnp.clip(values, -limit, limit).astype(kind)


def setup_inputs(seed: int = 0) -> dict:
    keys = jax.random.split(jax.random.key(seed), 7)
    slab = scatter_about(keys[0], (M, K), 1.0, 6.0, ((0, 4), (1, 32)))
    slab_mask = draw_slab_mask(jax.random.fold_in(keys[6], 71), 0)
    order = jax.random.permutation(keys[2], CONTRACT_TILES).astype(jnp.int32)
    integrals = scatter_about(keys[3], (STEPS, N_ROW * KP, N), K ** -0.5, 0.0625, ((1, 4), (2, 32)))
    integral_mask = set_ends((jax.random.randint(keys[4], (STEPS, N_ROW * PT, NTILES), 0, 4) < 3).astype(jnp.int32), jax.random.fold_in(keys[4], 1), 0, 1)
    row_owner = jax.random.randint(keys[5], (STEPS,), 0, N_ROW).astype(jnp.int32)
    return dict(slab=slab, slab_mask=slab_mask, order=order, integrals=integrals, integral_mask=integral_mask, row_owner=row_owner)


def tile_expand(mask):
    return jnp.repeat(jnp.repeat(mask, TW, axis=-2), TW, axis=-1)


def reference(slab, slab_mask, order, integrals, integral_mask, row_owner):
    masked_slab = slab * tile_expand(slab_mask).astype(jnp.bfloat16)
    tiles = masked_slab.reshape(M, CONTRACT_TILES, TW)
    ordered = jnp.take(tiles, order, axis=1).reshape(M, K)
    total = jnp.zeros((M, N), jnp.float32)
    for step in range(STEPS):
        owner = row_owner[step].astype(jnp.int32)
        panel = lax.dynamic_slice_in_dim(integrals[step], (owner * KP).astype(jnp.int32), KP, 0)
        panel_mask = lax.dynamic_slice_in_dim(integral_mask[step], (owner * PT).astype(jnp.int32), PT, 0)
        panel = panel * tile_expand(panel_mask).astype(jnp.bfloat16)
        total = total + jnp.dot(ordered[:, step * KP:(step + 1) * KP], panel, preferred_element_type=jnp.float32)
    return total.astype(jnp.bfloat16)
```

```python
import functools

import jax
import jax.numpy as jnp
from jax import lax
from jax.experimental import pallas as pl
from jax.experimental.pallas import tpu as pltpu
from jax.sharding import PartitionSpec as P

TW = 256
AXES = ("row", "col")
SIDE = 4
PAD = 16
CHUNKS = ((0, 2), (2, 4), (6, 4), (10, 4), (14, 2))
CALLS = ((0, 1, 2, 3), (4,))


def number(y, x, z, core):
    return ((y % 2) * 2 + core) * 2 * SIDE * SIDE + (y // 2) * SIDE * SIDE + x * SIDE + z


def pairs(target):
    out = []
    for y in range(SIDE):
        for x in range(SIDE):
            for z in range(SIDE):
                for core in range(2):
                    to = target(y, x, z, core)
                    if to is not None:
                        ty, tx, tz, tcore = to
                        out.append((number(y, x, z, core), number(ty % SIDE, tx % SIDE, tz % SIDE, tcore)))
    return out


def step_of(core):
    return 1 if core == 0 else -1


X_RING = pairs(lambda y, x, z, c: (y, x + step_of(c), z, c))
Z_RING = pairs(lambda y, x, z, c: (y, x, z + step_of(c), c))
Y_TWO = pairs(lambda y, x, z, c: (y + 2, x, z, c))
CORES = pairs(lambda y, x, z, c: (y, x, z, 1 - c))


def cores_on(plane):
    return pairs(lambda y, x, z, c: (y, x, z, 1 - c) if y % 2 == plane else None)


def send(array, where):
    return lax.ppermute(array, AXES, where)


def select_kernel(first, tiles, scalars, masks, mine_ref, swapped_ref, near_ref, far_ref):
    i, t = pl.program_id(0), pl.program_id(1)
    core = scalars[0]
    panel = scalars[1 + i]
    owner = scalars[3 + i]

    def emit(ref, half):
        for h in range(2):
            target = near_ref if h == half else far_ref
            for j in range(2):
                n = 2 * h + j
                keep = masks[panel * 64 + (first + t) * 4 + n].astype(jnp.float32)
                keep = jnp.full((TW, TW), keep, jnp.float32).astype(jnp.bfloat16)
                target[0, :, j * TW : (j + 1) * TW] = ref[0, :, n * TW : (n + 1) * TW] * keep

    for half in range(2):
        for own in range(2):

            @pl.when((core == half) & (owner == own))
            def _():
                emit(mine_ref if own else swapped_ref, half)


def select(first, tiles, scalars, masks, integrals, swapped):
    panels = swapped.shape[0]
    rows = tiles * TW
    half = integrals.shape[2] // 2
    out = jax.ShapeDtypeStruct((panels, rows, half), jnp.bfloat16)
    whole = integrals.shape[2]
    return pl.pallas_call(
        functools.partial(select_kernel, first, tiles),
        out_shape=(out, out),
        grid_spec=pltpu.PrefetchScalarGridSpec(
            num_scalar_prefetch=2,
            grid=(panels, tiles),
            in_specs=[
                pl.BlockSpec((1, TW, whole), lambda i, t, s, m: (s[1 + i], first + t, 0)),
                pl.BlockSpec((1, TW, whole), lambda i, t, s, m: (i, t, 0)),
            ],
            out_specs=[
                pl.BlockSpec((1, TW, half), lambda i, t, s, m: (i, t, 0)),
                pl.BlockSpec((1, TW, half), lambda i, t, s, m: (i, t, 0)),
            ],
        ),
        compiler_params=pltpu.CompilerParams(vmem_limit_bytes=24 * 2**20),
        cost_estimate=pl.CostEstimate(flops=0, bytes_accessed=panels * rows * whole * 6, transcendentals=0),
        name="select_panel",
    )(scalars, masks, integrals, swapped)


def matmul_kernel(chunks, shared, first, last, scalars, arr, slot, *refs):
    refs = list(refs)
    slabs = [refs.pop(0) for _ in range(8)]
    parts = [[refs.pop(0) for _ in range(4)] for _ in chunks]
    acc_in = None if first else refs.pop(0)
    out = refs.pop(0)
    out_right = refs.pop(0) if last else None
    lhs, rhs, extra, zvec, zsm, sem_l, sem_r, sem_e, sem_z = refs[:9]
    acc = refs[9] if last else out
    core = scalars[0]

    steps = []
    for c, (t0, nt) in enumerate(chunks):
        for s in range(2):
            for t in range(nt):
                steps.append((c, s, t0, t))

    extras = [
        pltpu.make_async_copy(slabs[a].at[:, pl.ds(3 * TW, PAD), :], extra.at[a], sem_e.at[a]) for a in range(8)
    ]
    for copy in extras:
        copy.start()

    base = 0
    for c, (t0, nt) in enumerate(chunks):
        for s in range(2):
            at = 0 if not shared else s

            def fetch(t, carry, c=c, s=s, t0=t0, base=base, at=at):
                i = base + t
                p = s * 16 + t0 + t
                for a in range(8):

                    @pl.when(arr[p] == a)
                    def _():
                        pltpu.make_async_copy(
                            slabs[a].at[slot[p], pl.ds(0, 3 * TW), :], lhs.at[i], sem_l.at[i]
                        ).start()

                row = pl.multiple_of(t * TW, TW)
                for role in range(2):
                    for k in range(2):

                        @pl.when((scalars[1 + s] == role) & (core == k))
                        def _():
                            near, far = parts[c][2 * role], parts[c][2 * role + 1]
                            pltpu.make_async_copy(near.at[at, pl.ds(row, TW), :], rhs.at[i, k], sem_r.at[i, 0]).start()
                            pltpu.make_async_copy(far.at[at, pl.ds(row, TW), :], rhs.at[i, 1 - k], sem_r.at[i, 1]).start()

                return carry

            lax.fori_loop(0, nt, fetch, 0)
            base += nt

    for copy in extras:
        copy.wait()
    for i in range(4):
        zvec[i] = extra[:, i, 0, 0:128].astype(jnp.float32).astype(jnp.int32)
    copy = pltpu.make_async_copy(zvec, zsm, sem_z)
    copy.start()
    copy.wait()
    if first:
        acc[...] = jnp.zeros_like(acc)
    else:
        acc[...] = acc_in[...]

    base = 0
    for c, (t0, nt) in enumerate(chunks):
        for s in range(2):

            def multiply(t, carry, s=s, t0=t0, base=base):
                i = base + t
                p = s * 16 + t0 + t
                zero = zsm[slot[p], arr[p], 0]
                pltpu.make_async_copy(slabs[0].at[0, pl.ds(0, 3 * TW), :], lhs.at[i], sem_l.at[i]).wait()
                for h in range(2):
                    pltpu.make_async_copy(parts[0][0].at[0, pl.ds(0, TW), :], rhs.at[i, h], sem_r.at[i, h]).wait()
                for h in range(2):
                    part = jnp.dot(lhs[i], rhs[i, h], preferred_element_type=jnp.float32)
                    for j in range(3):
                        at = jnp.where(j >= zero, j + 1, j)
                        rows = pl.ds(pl.multiple_of(at * TW, TW), TW)
                        acc[rows, h * 512 : (h + 1) * 512] += part[j * TW : (j + 1) * TW]
                return carry

            lax.fori_loop(0, nt, multiply, 0)
            base += nt
    if last:
        out[...] = acc[:, :512].astype(out.dtype)
        out_right[...] = acc[:, 512:].astype(out.dtype)


def matmul(chunks, shared, first, last, scalars, arr, slot, slabs, parts, acc):
    steps = sum(2 * nt for _, nt in chunks)
    rows = 4 * TW
    columns = 4 * TW
    if last:
        half = jax.ShapeDtypeStruct((rows, columns // 2), jnp.bfloat16)
        out = (half, half)
    else:
        out = (jax.ShapeDtypeStruct((rows, columns), jnp.float32),)
    flat = [ref for chunk in parts for ref in chunk]
    hbm = pl.BlockSpec(memory_space=pl.ANY)
    vmem = pl.BlockSpec(memory_space=pltpu.VMEM)
    scratch = [
        pltpu.VMEM((steps, 3 * TW, TW), jnp.bfloat16),
        pltpu.VMEM((steps, 2, TW, columns // 2), jnp.bfloat16),
        pltpu.VMEM((8, 4, PAD, TW), jnp.bfloat16),
        pltpu.VMEM((4, 8, 128), jnp.int32),
        pltpu.SMEM((4, 8, 128), jnp.int32),
        pltpu.SemaphoreType.DMA((steps,)),
        pltpu.SemaphoreType.DMA((steps, 2)),
        pltpu.SemaphoreType.DMA((8,)),
        pltpu.SemaphoreType.DMA,
    ]
    if last:
        scratch.append(pltpu.VMEM((rows, columns), jnp.float32))
    return pl.pallas_call(
        functools.partial(matmul_kernel, chunks, shared, first, last),
        out_shape=out,
        grid_spec=pltpu.PrefetchScalarGridSpec(
            num_scalar_prefetch=3,
            grid=(1,),
            in_specs=[hbm] * (8 + len(flat)) + ([] if first else [vmem]),
            out_specs=[vmem] * len(out),
            scratch_shapes=scratch,
        ),
        compiler_params=pltpu.CompilerParams(vmem_limit_bytes=56 * 2**20),
        cost_estimate=pl.CostEstimate(
            flops=steps * 2 * 3 * TW * TW * columns, bytes_accessed=steps * (3 * TW * TW + TW * columns) * 2, transcendentals=0
        ),
        name="multiply_chunks",
    )(scalars, arr, slot, *slabs, *flat, *([] if first else [acc]))


def run(planes, payload, arr, slot, integrals, masks, row_owner):
    row = lax.axis_index("row")
    core, plane = row % 2, row // 2
    shared = planes[0] == planes[1]
    whole = integrals.shape[2]

    if shared:
        here = planes[0]
        up = 1 if here == 0 else -1
        swap_raw = cores_on(here)
        over = pairs(lambda y, x, z, c: (y + (up if c == 0 else -up), x, z, c) if y % 2 == here else None)
        swap_got = cores_on(1 - here)
        numbers = [jnp.int32(0), jnp.int32(1)]
    else:
        swap_raw = CORES
        over = pairs(lambda y, x, z, c: (y ^ 1, x, z, c))
        swap_got = CORES
        numbers = [jnp.where(plane == planes[0], 0, 1).astype(jnp.int32)]
    owners = [(row_owner[n] % 2 == core).astype(jnp.int32) for n in numbers]
    if not shared:
        numbers, owners = numbers * 2, owners * 2
    select_scalars = jnp.stack([core.astype(jnp.int32), *numbers, *owners])
    roles = [(plane != planes[s]).astype(jnp.int32) for s in range(2)]
    matmul_scalars = jnp.stack([core.astype(jnp.int32), *roles])

    parts = []
    for t0, nt in CHUNKS:
        r0, n = t0 * TW, nt * TW
        if shared:
            raw = integrals[:, r0 : r0 + n, :]
        else:
            raw = lax.dynamic_slice(integrals, (numbers[0], jnp.int32(r0), jnp.int32(0)), (1, n, whole))
        swapped = send(raw, swap_raw)
        near, far = select(t0, nt, select_scalars, masks, integrals, swapped)
        got = send(near, over)
        parts.append([near, far, got])

    across = send(payload, Y_TWO)
    own, other = [payload], [across]
    for _ in range(SIDE - 1):
        own.append(send(own[-1], X_RING))
        other.append(send(other[-1], Z_RING))
    own, other = [jnp.stack(own)], [jnp.stack(other)]
    for _ in range(SIDE - 1):
        own.append(send(own[-1], Z_RING))
        other.append(send(other[-1], X_RING))
    slabs = own + other

    for part in parts:
        part.append(send(part[2], swap_got))

    acc = None
    for n, call in enumerate(CALLS):
        last = n == len(CALLS) - 1
        acc = matmul(
            [CHUNKS[c] for c in call], shared, n == 0, last, matmul_scalars, arr, slot, slabs, [parts[c] for c in call],
            None if n == 0 else acc[0],
        )
    left, right = acc
    if shared:
        back = send(right, pairs(lambda y, x, z, c: (y + 2, x, z, c) if y % 2 != here else None))
        right = jnp.where(plane == here, right, back)
    return jnp.concatenate([left, right], axis=1)


def per_device(slab, slab_mask, order, integrals, integral_mask, row_owner):
    row, col = lax.axis_index("row"), lax.axis_index("col")
    core = row % 2
    zero = jnp.sum(jnp.arange(4, dtype=jnp.int32) * (1 - slab_mask[:, 0]))
    tiles = slab.reshape(4, TW, TW)
    kept = jnp.where(jnp.arange(3, dtype=jnp.int32)[:, None, None] >= zero, tiles[1:], tiles[:3])
    payload = jnp.concatenate(
        [kept.reshape(3 * TW, TW), jnp.full((PAD, TW), zero.astype(jnp.float32), jnp.float32).astype(jnp.bfloat16)], axis=0
    )

    high, x, z = col // (SIDE * SIDE), (col // SIDE) % SIDE, col % SIDE
    high_q, x_q, z_q = order // (SIDE * SIDE), (order // SIDE) % SIDE, order % SIDE
    sign = jnp.where(core == 0, 1, -1)
    dx, dz = (sign * (x - x_q)) % SIDE, (sign * (z - z_q)) % SIDE
    own = high_q == high
    arr = jnp.where(own, dz, 4 + dx).astype(jnp.int32)
    slot = jnp.where(own, dx, dz).astype(jnp.int32)

    swapped = send(integral_mask, CORES)
    mine = (row_owner % 2 == core)[:, None, None]
    masks = jnp.where(mine, integral_mask, swapped).reshape(-1)

    planes = row_owner // 2
    branches = [functools.partial(run, (a, b)) for a in range(2) for b in range(2)]
    return lax.switch(planes[0] * 2 + planes[1], branches, payload, arr, slot, integrals, masks, row_owner)


def solution(mesh):
    return jax.shard_map(
        per_device,
        mesh=mesh,
        in_specs=(
            P("row", "col"),
            P("row", "col"),
            P(),
            P(None, "row", "col"),
            P(None, "row", "col"),
            P(),
        ),
        out_specs=P("row", "col"),
        check_vma=False,
    )
```

```python
import functools

import jax
import jax.numpy as jnp
from jax import lax
from jax.experimental import pallas as pl
from jax.experimental.pallas import tpu as pltpu
from jax.sharding import PartitionSpec as P

TW = 256
AXES = ("row", "col")
SIDE = 4
PAD = 16
PIECES = ((0, 4), (4, 4), (8, 4), (12, 4))
HELD = ((0, 4), (4, 4), (8, 8), (8, 8))
STEP = 2


def number(y, x, z, core):
    return ((y % 2) * 2 + core) * 2 * SIDE * SIDE + (y // 2) * SIDE * SIDE + x * SIDE + z


def pairs(target):
    out = []
    for y in range(SIDE):
        for x in range(SIDE):
            for z in range(SIDE):
                for core in range(2):
                    to = target(y, x, z, core)
                    if to is not None:
                        ty, tx, tz, tcore = to
                        out.append((number(y, x, z, core), number(ty % SIDE, tx % SIDE, tz % SIDE, tcore)))
    return out


def step_of(core):
    return 1 if core == 0 else -1


X_RING = pairs(lambda y, x, z, c: (y, x + step_of(c), z, c))
Z_RING = pairs(lambda y, x, z, c: (y, x, z + step_of(c), c))
Y_TWO = pairs(lambda y, x, z, c: (y + 2, x, z, c))
CORES = pairs(lambda y, x, z, c: (y, x, z, 1 - c))


def cores_on(plane):
    return pairs(lambda y, x, z, c: (y, x, z, 1 - c) if y % 2 == plane else None)


def send(array, where):
    return lax.ppermute(array, AXES, where)


def mask_kernel(first, scalars, masks, slot_ref, out_ref):
    i, g = pl.program_id(0), pl.program_id(1)

    def tile(n, carry):
        rows = pl.ds(pl.multiple_of(n // 4 * TW, TW), TW)
        lanes = pl.ds(pl.multiple_of(n % 4 * TW, TW), TW)
        keep = masks[scalars[i] * 64 + (first + g * STEP) * 4 + n].astype(jnp.float32)
        keep = jnp.full((TW, TW), keep, jnp.float32).astype(jnp.bfloat16)
        out_ref[0, rows, lanes] = slot_ref[0, rows, lanes] * keep
        return carry

    lax.fori_loop(0, STEP * 4, tile, 0)


def mask_piece(first, tiles, panels, numbers, masks, integrals):
    rows, whole = STEP * TW, integrals.shape[2]
    return pl.pallas_call(
        functools.partial(mask_kernel, first),
        out_shape=jax.ShapeDtypeStruct((panels, tiles * TW, whole), jnp.bfloat16),
        grid_spec=pltpu.PrefetchScalarGridSpec(
            num_scalar_prefetch=2,
            grid=(panels, tiles // STEP),
            in_specs=[pl.BlockSpec((1, rows, whole), lambda i, g, s, m: (s[i], first // STEP + g, 0))],
            out_specs=pl.BlockSpec((1, rows, whole), lambda i, g, s, m: (i, g, 0)),
        ),
        compiler_params=pltpu.CompilerParams(vmem_limit_bytes=16 * 2**20),
        cost_estimate=pl.CostEstimate(flops=0, bytes_accessed=panels * tiles * TW * whole * 4, transcendentals=0),
        name="mask_piece",
    )(numbers, masks, integrals)


def near_kernel(scalars, mine_ref, swapped_ref, out_ref):
    owner = scalars[1 + pl.program_id(0)]

    def copy(ref):
        def some(n, carry):
            rows = pl.ds(pl.multiple_of(n * 128, 128), 128)
            out_ref[0, rows, :] = ref[0, rows, :]
            return carry

        lax.fori_loop(0, STEP * 2, some, 0)

    @pl.when(owner == 1)
    def _():
        copy(mine_ref)

    @pl.when(owner == 0)
    def _():
        copy(swapped_ref)


def near_half(first, tiles, scalars, mine, swapped):
    panels, _, whole = mine.shape
    rows, half = STEP * TW, whole // 2
    first = first // STEP
    return pl.pallas_call(
        near_kernel,
        out_shape=jax.ShapeDtypeStruct((panels, tiles * TW, half), jnp.bfloat16),
        grid_spec=pltpu.PrefetchScalarGridSpec(
            num_scalar_prefetch=1,
            grid=(panels, tiles // STEP),
            in_specs=[
                pl.BlockSpec((1, rows, half), lambda i, g, s: (i, (first + g) * s[1 + i], s[0])),
                pl.BlockSpec((1, rows, half), lambda i, g, s: (i, (first + g) * (1 - s[1 + i]), s[0])),
            ],
            out_specs=pl.BlockSpec((1, rows, half), lambda i, g, s: (i, g, 0)),
        ),
        compiler_params=pltpu.CompilerParams(vmem_limit_bytes=16 * 2**20),
        cost_estimate=pl.CostEstimate(flops=0, bytes_accessed=panels * tiles * TW * half * 4, transcendentals=0),
        name="near_half",
    )(scalars, mine, swapped)


def zero_kernel(names, *refs):
    count = len(names)
    slabs, out, extra, sems = refs[:count], refs[count], refs[count + 1], refs[count + 2]
    copies = [pltpu.make_async_copy(ref.at[:, pl.ds(3 * TW, PAD), :], extra.at[a], sems.at[a]) for a, ref in zip(names, slabs)]
    for copy in copies:
        copy.start()
    for copy in copies:
        copy.wait()
    lane = lax.broadcasted_iota(jnp.int32, (8, 128), 1)
    found = jnp.zeros((8, 128), jnp.int32)
    for i in range(4):
        found = jnp.where(lane == i, extra[:, i, 0, 0:128].astype(jnp.float32).astype(jnp.int32), found)
    out[...] = found


def zero_places(names, slabs):
    return pl.pallas_call(
        functools.partial(zero_kernel, names),
        out_shape=jax.ShapeDtypeStruct((8, 128), jnp.int32),
        in_specs=[pl.BlockSpec(memory_space=pl.ANY)] * len(slabs),
        out_specs=pl.BlockSpec(memory_space=pltpu.VMEM),
        scratch_shapes=[pltpu.VMEM((8, 4, PAD, TW), jnp.bfloat16), pltpu.SemaphoreType.DMA((8,))],
        compiler_params=pltpu.CompilerParams(vmem_limit_bytes=8 * 2**20),
        name="zero_places",
    )(*slabs)


def matmul_kernel(names, pieces, shared, first, last, scalars, arr, slot, todo, zeros, *refs):
    refs = list(refs)
    slabs = [refs.pop(0) for _ in names]
    parts = [[refs.pop(0) for _ in range(4)] for _ in pieces]
    acc_in = None if first else refs.pop(0)
    out, lhs, rhs, sem_l, sem_r = refs[:5]
    acc = out if last is None else refs[5]
    core = scalars[0]
    halves = range(2) if last is None else (last,)

    begin = pieces[0][0]
    span = sum(nt for _, nt in pieces)

    base = 0
    for s in range(2):
        at = s if shared else 0
        for (t0, nt), (mine, swapped, got, other) in zip(pieces, parts):
            ahead = t0 - dict(zip(PIECES, HELD))[t0, nt][0]

            def fetch(t, carry, s=s, t0=t0, at=at, base=base, ahead=ahead, mine=mine, swapped=swapped, got=got, other=other):
                n, p = base + t, s * 16 + t0 + t
                sent = pl.ds(pl.multiple_of(t * TW, TW), TW)
                held = pl.ds(pl.multiple_of((ahead + t) * TW, TW), TW)

                @pl.when(todo[p] == 1)
                def _():
                    for m, a in enumerate(names):

                        @pl.when(arr[p] == a)
                        def _():
                            pltpu.make_async_copy(slabs[m].at[slot[p], pl.ds(0, 3 * TW), :], lhs.at[n], sem_l.at[n]).start()

                    for place, ref in ((0, mine), (1, swapped)):

                        @pl.when(scalars[1 + s] == place)
                        def _():
                            for h in halves:
                                pltpu.make_async_copy(
                                    ref.at[at, held, pl.ds(h * 512, 512)], rhs.at[n, h], sem_r.at[n, h]
                                ).start()

                    @pl.when(scalars[1 + s] == 2)
                    def _():
                        for h in halves:
                            for near, ref in ((1, got), (0, other)):

                                @pl.when(core == (h if near else 1 - h))
                                def _():
                                    pltpu.make_async_copy(ref.at[at, sent, :], rhs.at[n, h], sem_r.at[n, h]).start()

                return carry

            lax.fori_loop(0, nt, fetch, 0)
            base += nt

    if first:
        acc[...] = jnp.zeros_like(acc)
    elif last is None:
        acc[...] = acc_in[...]
    else:
        acc[...] = acc_in[:, last * 512 : (last + 1) * 512]

    def multiply(n, carry):
        p = n // span * 16 + begin + n % span

        @pl.when(todo[p] == 1)
        def _():
            zero = zeros[arr[p], slot[p]]
            pltpu.make_async_copy(slabs[0].at[0, pl.ds(0, 3 * TW), :], lhs.at[n], sem_l.at[n]).wait()
            for h in halves:
                pltpu.make_async_copy(parts[0][2].at[0, pl.ds(0, TW), :], rhs.at[n, h], sem_r.at[n, h]).wait()
            for h in halves:
                lanes = slice(h * 512, (h + 1) * 512) if last is None else slice(None)
                part = jnp.dot(lhs[n], rhs[n, h], preferred_element_type=jnp.float32)
                for j in range(3):
                    to = jnp.where(j >= zero, j + 1, j)
                    rows = pl.ds(pl.multiple_of(to * TW, TW), TW)
                    acc[rows, lanes] += part[j * TW : (j + 1) * TW]

        return carry

    lax.fori_loop(0, 2 * span, multiply, 0)
    if last is not None:
        out[...] = acc[...].astype(out.dtype)


def matmul(names, pieces, shared, first, last, scalars, arr, slot, todo, zeros, slabs, parts, acc):
    steps = sum(2 * nt for _, nt in pieces)
    rows = columns = 4 * TW
    if last is None:
        out = jax.ShapeDtypeStruct((rows, columns), jnp.float32)
    else:
        out = jax.ShapeDtypeStruct((rows, columns // 2), jnp.bfloat16)
    flat = [ref for part in parts for ref in part]
    hbm = pl.BlockSpec(memory_space=pl.ANY)
    vmem = pl.BlockSpec(memory_space=pltpu.VMEM)
    scratch = [
        pltpu.VMEM((steps, 3 * TW, TW), jnp.bfloat16),
        pltpu.VMEM((steps, 2, TW, columns // 2), jnp.bfloat16),
        pltpu.SemaphoreType.DMA((steps,)),
        pltpu.SemaphoreType.DMA((steps, 2)),
    ]
    if last is not None:
        scratch.append(pltpu.VMEM((rows, columns // 2), jnp.float32))
    return pl.pallas_call(
        functools.partial(matmul_kernel, names, pieces, shared, first, last),
        out_shape=out,
        grid_spec=pltpu.PrefetchScalarGridSpec(
            num_scalar_prefetch=5,
            grid=(1,),
            in_specs=[hbm] * (len(slabs) + len(flat)) + ([] if first else [vmem]),
            out_specs=vmem,
            scratch_shapes=scratch,
        ),
        compiler_params=pltpu.CompilerParams(vmem_limit_bytes=52 * 2**20),
        cost_estimate=pl.CostEstimate(
            flops=steps * TW * TW * columns * 4, bytes_accessed=steps * (3 * TW * TW + TW * columns), transcendentals=0
        ),
        name="multiply_pieces",
    )(scalars, arr, slot, todo, zeros, *slabs, *flat, *([] if first else [acc]))


def after(values, others):
    return lax.optimization_barrier((*values, *others))[: len(values)]


def run(planes, payload, arr, slot, integrals, masks, row_owner):
    row = lax.axis_index("row")
    core, plane = (row % 2).astype(jnp.int32), row // 2
    shared = planes[0] == planes[1]
    here = planes[0]

    if shared:
        up = 1 if here == 0 else -1
        swap_mine = cores_on(here)
        over = pairs(lambda y, x, z, c: (y + (up if c == 0 else -up), x, z, c) if y % 2 == here else None)
        swap_got = cores_on(1 - here)
        panels = 2
        numbers = jnp.arange(2, dtype=jnp.int32)
        owners = (row_owner % 2 == core).astype(jnp.int32)
    else:
        swap_mine = CORES
        over = pairs(lambda y, x, z, c: (y ^ 1, x, z, c))
        swap_got = CORES
        panels = 1
        held = jnp.where(plane == here, 0, 1).astype(jnp.int32)
        numbers = held[None]
        owners = jnp.where(plane == here, row_owner[0], row_owner[1])[None] % 2 == core
        owners = owners.astype(jnp.int32)
    near_scalars = jnp.concatenate([core[None], owners])
    places = [jnp.where(plane != planes[s], 2, 1 - (row_owner[s] % 2 == core).astype(jnp.int32)) for s in range(2)]
    matmul_scalars = jnp.stack([core, *places]).astype(jnp.int32)

    x_first, z_first = [payload, send(payload, X_RING)], [send(payload, Y_TWO)]

    def prepare(c, waits):
        mine = mask_piece(*HELD[c], panels, waits, masks, integrals)
        return mine, send(mine, swap_mine)

    def near_of(c, scalars):
        return near_half(PIECES[c][0] - HELD[c][0], PIECES[c][1], scalars, *masked[c])

    masked = [prepare(0, numbers)]
    masked.append(prepare(1, *after((numbers,), (masked[0][0],))))
    near = [near_of(0, *after((near_scalars,), (masked[1][0],)))]
    got, other = [send(*after((near[0],), (x_first[1], z_first[0])), over)], []
    x_first.append(send(*after((x_first[1],), (near[0],)), X_RING))
    z_first.append(send(*after((z_first[0],), (near[0],)), Z_RING))
    near.append(near_of(1, near_scalars))
    x_first.append(send(x_first[2], X_RING))
    z_first.append(send(*after((z_first[1],), (near[1],)), Z_RING))
    z_first.append(send(z_first[2], Z_RING))
    own, foreign = [jnp.stack(x_first)], [jnp.stack(z_first)]
    for n in range(3):
        ready = [got[n], *other[n - 1 : n], *near[n + 1 :]]
        x_now, z_now, near_now, waits = after((own[n], foreign[n], near[n + 1], numbers), ready)
        got.append(send(near_now, over))
        own.append(send(x_now, Z_RING))
        foreign.append(send(z_now, X_RING))
        other.append(send(got[n], swap_got))
        if n == 0:
            masked += [prepare(2, waits)] * 2
            near += [near_of(2, near_scalars), near_of(3, near_scalars)]

    parts = [pair + part for pair, part in zip(masked, zip(got, other))]
    piece_of = jnp.arange(32, dtype=jnp.int32) % 16 // 4
    early = ((piece_of < 3) & (arr % 4 < 3)).astype(jnp.int32)
    middle = jnp.where(piece_of < 3, 1 - early, 0)
    late = (piece_of == 3).astype(jnp.int32)
    static = (matmul_scalars, arr, slot)
    slabs = own[:3] + foreign[:3]
    names = (0, 1, 2, 4, 5, 6)
    zeros = zero_places(names, slabs)
    acc = matmul(names, PIECES[:3], shared, True, None, *static, early, zeros, slabs, parts[:3], None)
    other.append(send(*after((got[3],), (acc,)), swap_got))
    parts.append(masked[3] + (got[3], other[3]))
    slabs = own + foreign
    names = tuple(range(8))
    zeros = zero_places(names, slabs)
    acc = matmul(names, PIECES[:3], shared, False, None, *static, middle, zeros, slabs, parts[:3], acc)
    right = matmul(names, PIECES[3:], shared, False, 1, *static, late, zeros, slabs, parts[3:], acc)
    left = matmul(names, PIECES[3:], shared, False, 0, *static, late, zeros, slabs, parts[3:], acc)
    if shared:
        back = send(right, pairs(lambda y, x, z, c: (y + 2, x, z, c) if y % 2 != here else None))
        right = jnp.where(plane == here, right, back)
    return jnp.concatenate([left, right], axis=1)


def per_device(slab, slab_mask, order, integrals, integral_mask, row_owner):
    row, col = lax.axis_index("row"), lax.axis_index("col")
    core = row % 2
    zero = jnp.sum(jnp.arange(4, dtype=jnp.int32) * (1 - slab_mask[:, 0]))
    tiles = slab.reshape(4, TW, TW)
    kept = jnp.where(jnp.arange(3, dtype=jnp.int32)[:, None, None] >= zero, tiles[1:], tiles[:3])
    payload = jnp.concatenate(
        [kept.reshape(3 * TW, TW), jnp.full((PAD, TW), zero.astype(jnp.float32), jnp.float32).astype(jnp.bfloat16)], axis=0
    )

    high, x, z = col // (SIDE * SIDE), (col // SIDE) % SIDE, col % SIDE
    high_q, x_q, z_q = order // (SIDE * SIDE), (order // SIDE) % SIDE, order % SIDE
    sign = jnp.where(core == 0, 1, -1)
    dx, dz = (sign * (x - x_q)) % SIDE, (sign * (z - z_q)) % SIDE
    own = high_q == high
    arr = jnp.where(own, dz, 4 + dx).astype(jnp.int32)
    slot = jnp.where(own, dx, dz).astype(jnp.int32)

    masks = integral_mask.reshape(-1)
    planes = row_owner // 2
    branches = [functools.partial(run, (a, b)) for a in range(2) for b in range(2)]
    return lax.switch(planes[0] * 2 + planes[1], branches, payload, arr, slot, integrals, masks, row_owner)


def solution(mesh):
    return jax.shard_map(
        per_device,
        mesh=mesh,
        in_specs=(
            P("row", "col"),
            P("row", "col"),
            P(),
            P(None, "row", "col"),
            P(None, "row", "col"),
            P(),
        ),
        out_specs=P("row", "col"),
        check_vma=False,
    )
```

```python
import functools

import jax
import jax.numpy as jnp
from jax import lax
from jax.experimental import pallas as pl
from jax.experimental.pallas import tpu as pltpu
from jax.sharding import PartitionSpec as P

TW = 256
AXES = ("row", "col")
SIDE = 4
PAD = 16
PIECES = ((0, 4), (4, 4), (8, 4), (12, 4))
HELD = ((0, 4), (4, 4), (8, 8), (8, 8))
STEP = 2


def number(y, x, z, core):
    return ((y % 2) * 2 + core) * 2 * SIDE * SIDE + (y // 2) * SIDE * SIDE + x * SIDE + z


def pairs(target):
    out = []
    for y in range(SIDE):
        for x in range(SIDE):
            for z in range(SIDE):
                for core in range(2):
                    to = target(y, x, z, core)
                    if to is not None:
                        ty, tx, tz, tcore = to
                        out.append((number(y, x, z, core), number(ty % SIDE, tx % SIDE, tz % SIDE, tcore)))
    return out


def step_of(core):
    return 1 if core == 0 else -1


X_RING = pairs(lambda y, x, z, c: (y, x + step_of(c), z, c))
Z_RING = pairs(lambda y, x, z, c: (y, x, z + step_of(c), c))
Y_TWO = pairs(lambda y, x, z, c: (y + 2, x, z, c))
CORES = pairs(lambda y, x, z, c: (y, x, z, 1 - c))


def cores_on(plane):
    return pairs(lambda y, x, z, c: (y, x, z, 1 - c) if y % 2 == plane else None)


def send(array, where):
    return lax.ppermute(array, AXES, where)


def mask_kernel(first, scalars, masks, slot_ref, out_ref):
    i, g = pl.program_id(0), pl.program_id(1)

    def tile(n, carry):
        rows = pl.ds(pl.multiple_of(n // 4 * TW, TW), TW)
        lanes = pl.ds(pl.multiple_of(n % 4 * TW, TW), TW)
        keep = masks[scalars[i] * 64 + (first + g * STEP) * 4 + n].astype(jnp.float32)
        keep = jnp.full((TW, TW), keep, jnp.float32).astype(jnp.bfloat16)
        out_ref[0, rows, lanes] = slot_ref[0, rows, lanes] * keep
        return carry

    lax.fori_loop(0, STEP * 4, tile, 0)


def mask_piece(first, tiles, panels, numbers, masks, integrals):
    rows, whole = STEP * TW, integrals.shape[2]
    return pl.pallas_call(
        functools.partial(mask_kernel, first),
        out_shape=jax.ShapeDtypeStruct((panels, tiles * TW, whole), jnp.bfloat16),
        grid_spec=pltpu.PrefetchScalarGridSpec(
            num_scalar_prefetch=2,
            grid=(panels, tiles // STEP),
            in_specs=[pl.BlockSpec((1, rows, whole), lambda i, g, s, m: (s[i], first // STEP + g, 0))],
            out_specs=pl.BlockSpec((1, rows, whole), lambda i, g, s, m: (i, g, 0)),
        ),
        compiler_params=pltpu.CompilerParams(vmem_limit_bytes=16 * 2**20),
        cost_estimate=pl.CostEstimate(flops=0, bytes_accessed=panels * tiles * TW * whole * 4, transcendentals=0),
        name="mask_piece",
    )(numbers, masks, integrals)


def near_kernel(scalars, mine_ref, swapped_ref, out_ref):
    owner = scalars[1 + pl.program_id(0)]

    def copy(ref):
        def some(n, carry):
            rows = pl.ds(pl.multiple_of(n * 128, 128), 128)
            out_ref[0, rows, :] = ref[0, rows, :]
            return carry

        lax.fori_loop(0, STEP * 2, some, 0)

    @pl.when(owner == 1)
    def _():
        copy(mine_ref)

    @pl.when(owner == 0)
    def _():
        copy(swapped_ref)


def near_half(first, tiles, scalars, mine, swapped):
    panels, _, whole = mine.shape
    rows, half = STEP * TW, whole // 2
    first = first // STEP
    return pl.pallas_call(
        near_kernel,
        out_shape=jax.ShapeDtypeStruct((panels, tiles * TW, half), jnp.bfloat16),
        grid_spec=pltpu.PrefetchScalarGridSpec(
            num_scalar_prefetch=1,
            grid=(panels, tiles // STEP),
            in_specs=[
                pl.BlockSpec((1, rows, half), lambda i, g, s: (i, (first + g) * s[1 + i], s[0])),
                pl.BlockSpec((1, rows, half), lambda i, g, s: (i, (first + g) * (1 - s[1 + i]), s[0])),
            ],
            out_specs=pl.BlockSpec((1, rows, half), lambda i, g, s: (i, g, 0)),
        ),
        compiler_params=pltpu.CompilerParams(vmem_limit_bytes=16 * 2**20),
        cost_estimate=pl.CostEstimate(flops=0, bytes_accessed=panels * tiles * TW * half * 4, transcendentals=0),
        name="near_half",
    )(scalars, mine, swapped)


def zero_kernel(names, *refs):
    count = len(names)
    slabs, out, extra, sems = refs[:count], refs[count], refs[count + 1], refs[count + 2]
    copies = [pltpu.make_async_copy(ref.at[:, pl.ds(3 * TW, PAD), :], extra.at[a], sems.at[a]) for a, ref in zip(names, slabs)]
    for copy in copies:
        copy.start()
    for copy in copies:
        copy.wait()
    lane = lax.broadcasted_iota(jnp.int32, (8, 128), 1)
    found = jnp.zeros((8, 128), jnp.int32)
    for i in range(4):
        found = jnp.where(lane == i, extra[:, i, 0, 0:128].astype(jnp.float32).astype(jnp.int32), found)
    out[...] = found


def zero_places(names, slabs):
    return pl.pallas_call(
        functools.partial(zero_kernel, names),
        out_shape=jax.ShapeDtypeStruct((8, 128), jnp.int32),
        in_specs=[pl.BlockSpec(memory_space=pl.ANY)] * len(slabs),
        out_specs=pl.BlockSpec(memory_space=pltpu.VMEM),
        scratch_shapes=[pltpu.VMEM((8, 4, PAD, TW), jnp.bfloat16), pltpu.SemaphoreType.DMA((8,))],
        compiler_params=pltpu.CompilerParams(vmem_limit_bytes=8 * 2**20),
        name="zero_places",
    )(*slabs)


def matmul_kernel(names, pieces, shared, first, last, scalars, arr, slot, todo, zeros, *refs):
    refs = list(refs)
    slabs = [refs.pop(0) for _ in names]
    parts = [[refs.pop(0) for _ in range(4)] for _ in pieces]
    acc_in = None if first else refs.pop(0)
    out, lhs, rhs, sem_l, sem_r = refs[:5]
    acc = out if last is None else refs[5]
    core = scalars[0]
    halves = range(2) if last is None else (last,)

    begin = pieces[0][0]
    span = sum(nt for _, nt in pieces)

    base = 0
    for s in range(2):
        at = s if shared else 0
        for (t0, nt), (mine, swapped, got, other) in zip(pieces, parts):
            ahead = t0 - dict(zip(PIECES, HELD))[t0, nt][0]

            def fetch(t, carry, s=s, t0=t0, at=at, base=base, ahead=ahead, mine=mine, swapped=swapped, got=got, other=other):
                n, p = base + t, s * 16 + t0 + t
                sent = pl.ds(pl.multiple_of(t * TW, TW), TW)
                held = pl.ds(pl.multiple_of((ahead + t) * TW, TW), TW)

                @pl.when(todo[p] == 1)
                def _():
                    for m, a in enumerate(names):

                        @pl.when(arr[p] == a)
                        def _():
                            pltpu.make_async_copy(slabs[m].at[slot[p], pl.ds(0, 3 * TW), :], lhs.at[n], sem_l.at[n]).start()

                    for place, ref in ((0, mine), (1, swapped)):

                        @pl.when(scalars[1 + s] == place)
                        def _():
                            for h in halves:
                                pltpu.make_async_copy(
                                    ref.at[at, held, pl.ds(h * 512, 512)], rhs.at[n, h], sem_r.at[n, h]
                                ).start()

                    @pl.when(scalars[1 + s] == 2)
                    def _():
                        for h in halves:
                            for near, ref in ((1, got), (0, other)):

                                @pl.when(core == (h if near else 1 - h))
                                def _():
                                    pltpu.make_async_copy(ref.at[at, sent, :], rhs.at[n, h], sem_r.at[n, h]).start()

                return carry

            lax.fori_loop(0, nt, fetch, 0)
            base += nt

    def by_rows(write):
        def some(r, carry):
            write(pl.ds(pl.multiple_of(r * 64, 64), 64))
            return carry

        lax.fori_loop(0, 16, some, 0)

    def fill(rows):
        if first:
            acc[rows, :] = jnp.zeros((64, acc.shape[1]), jnp.float32)
        elif last is None:
            acc[rows, :] = acc_in[rows, :]
        else:
            acc[rows, :] = acc_in[rows, last * 512 : (last + 1) * 512]

    by_rows(fill)

    def multiply(n, carry):
        p = n // span * 16 + begin + n % span

        @pl.when(todo[p] == 1)
        def _():
            zero = zeros[arr[p], slot[p]]
            pltpu.make_async_copy(slabs[0].at[0, pl.ds(0, 3 * TW), :], lhs.at[n], sem_l.at[n]).wait()
            for h in halves:
                pltpu.make_async_copy(parts[0][2].at[0, pl.ds(0, TW), :], rhs.at[n, h], sem_r.at[n, h]).wait()
            for h in halves:
                lanes = slice(h * 512, (h + 1) * 512) if last is None else slice(None)
                part = jnp.dot(lhs[n], rhs[n, h], preferred_element_type=jnp.float32)
                for j in range(3):
                    to = jnp.where(j >= zero, j + 1, j)
                    rows = pl.ds(pl.multiple_of(to * TW, TW), TW)
                    acc[rows, lanes] += part[j * TW : (j + 1) * TW]

        return carry

    lax.fori_loop(0, 2 * span, multiply, 0)
    if last is not None:

        def finish(rows):
            out[rows, :] = acc[rows, :].astype(out.dtype)

        by_rows(finish)


def matmul(names, pieces, shared, first, last, scalars, arr, slot, todo, zeros, slabs, parts, acc):
    steps = sum(2 * nt for _, nt in pieces)
    rows = columns = 4 * TW
    if last is None:
        out = jax.ShapeDtypeStruct((rows, columns), jnp.float32)
    else:
        out = jax.ShapeDtypeStruct((rows, columns // 2), jnp.bfloat16)
    flat = [ref for part in parts for ref in part]
    hbm = pl.BlockSpec(memory_space=pl.ANY)
    vmem = pl.BlockSpec(memory_space=pltpu.VMEM)
    scratch = [
        pltpu.VMEM((steps, 3 * TW, TW), jnp.bfloat16),
        pltpu.VMEM((steps, 2, TW, columns // 2), jnp.bfloat16),
        pltpu.SemaphoreType.DMA((steps,)),
        pltpu.SemaphoreType.DMA((steps, 2)),
    ]
    if last is not None:
        scratch.append(pltpu.VMEM((rows, columns // 2), jnp.float32))
    return pl.pallas_call(
        functools.partial(matmul_kernel, names, pieces, shared, first, last),
        out_shape=out,
        grid_spec=pltpu.PrefetchScalarGridSpec(
            num_scalar_prefetch=5,
            grid=(1,),
            in_specs=[hbm] * (len(slabs) + len(flat)) + ([] if first else [vmem]),
            out_specs=vmem,
            scratch_shapes=scratch,
        ),
        compiler_params=pltpu.CompilerParams(vmem_limit_bytes=52 * 2**20),
        cost_estimate=pl.CostEstimate(
            flops=steps * TW * TW * columns * 4, bytes_accessed=steps * (3 * TW * TW + TW * columns), transcendentals=0
        ),
        name="multiply_pieces",
    )(scalars, arr, slot, todo, zeros, *slabs, *flat, *([] if first else [acc]))


def after(values, others):
    return lax.optimization_barrier((*values, *others))[: len(values)]


def run(planes, payload, arr, slot, integrals, masks, row_owner):
    row = lax.axis_index("row")
    core, plane = (row % 2).astype(jnp.int32), row // 2
    shared = planes[0] == planes[1]
    here = planes[0]

    if shared:
        up = 1 if here == 0 else -1
        swap_mine = cores_on(here)
        over = pairs(lambda y, x, z, c: (y + (up if c == 0 else -up), x, z, c) if y % 2 == here else None)
        swap_got = cores_on(1 - here)
        panels = 2
        numbers = jnp.arange(2, dtype=jnp.int32)
        owners = (row_owner % 2 == core).astype(jnp.int32)
    else:
        swap_mine = CORES
        over = pairs(lambda y, x, z, c: (y ^ 1, x, z, c))
        swap_got = CORES
        panels = 1
        held = jnp.where(plane == here, 0, 1).astype(jnp.int32)
        numbers = held[None]
        owners = jnp.where(plane == here, row_owner[0], row_owner[1])[None] % 2 == core
        owners = owners.astype(jnp.int32)
    near_scalars = jnp.concatenate([core[None], owners])
    places = [jnp.where(plane != planes[s], 2, 1 - (row_owner[s] % 2 == core).astype(jnp.int32)) for s in range(2)]
    matmul_scalars = jnp.stack([core, *places]).astype(jnp.int32)

    x_first, z_first = [payload, send(payload, X_RING)], [send(payload, Y_TWO)]

    def prepare(c, waits):
        mine = mask_piece(*HELD[c], panels, waits, masks, integrals)
        return mine, send(mine, swap_mine)

    def near_of(c, scalars):
        return near_half(PIECES[c][0] - HELD[c][0], PIECES[c][1], scalars, *masked[c])

    masked = [prepare(0, numbers)]
    masked.append(prepare(1, *after((numbers,), (masked[0][0],))))
    near = [near_of(0, *after((near_scalars,), (masked[1][0],)))]
    got, other = [send(*after((near[0],), (x_first[1], z_first[0])), over)], []
    x_first.append(send(*after((x_first[1],), (near[0],)), X_RING))
    z_first.append(send(*after((z_first[0],), (near[0],)), Z_RING))
    near.append(near_of(1, near_scalars))
    x_first.append(send(x_first[2], X_RING))
    z_first.append(send(*after((z_first[1],), (near[1],)), Z_RING))
    z_first.append(send(z_first[2], Z_RING))
    own, foreign = [jnp.stack(x_first)], [jnp.stack(z_first)]
    for n in range(3):
        ready = [got[n], *other[n - 1 : n], *near[n + 1 :]]
        x_now, z_now, near_now, waits = after((own[n], foreign[n], near[n + 1], numbers), ready)
        got.append(send(near_now, over))
        own.append(send(x_now, Z_RING))
        foreign.append(send(z_now, X_RING))
        other.append(send(got[n], swap_got))
        if n == 0:
            masked += [prepare(2, waits)] * 2
            near += [near_of(2, near_scalars), near_of(3, near_scalars)]

    parts = [pair + part for pair, part in zip(masked, zip(got, other))]
    piece_of = jnp.arange(32, dtype=jnp.int32) % 16 // 4
    early = ((piece_of < 3) & (arr % 4 < 3)).astype(jnp.int32)
    middle = jnp.where(piece_of < 3, 1 - early, 0)
    late = (piece_of == 3).astype(jnp.int32)
    static = (matmul_scalars, arr, slot)
    slabs = own[:3] + foreign[:3]
    names = (0, 1, 2, 4, 5, 6)
    zeros = zero_places(names, slabs)
    acc = matmul(names, PIECES[:3], shared, True, None, *static, early, zeros, slabs, parts[:3], None)
    other.append(send(*after((got[3],), (acc,)), swap_got))
    parts.append(masked[3] + (got[3], other[3]))
    slabs = own + foreign
    names = tuple(range(8))
    zeros = zero_places(names, slabs)
    acc = matmul(names, PIECES[:3], shared, False, None, *static, middle, zeros, slabs, parts[:3], acc)
    right = matmul(names, PIECES[3:], shared, False, 1, *static, late, zeros, slabs, parts[3:], acc)
    left = matmul(names, PIECES[3:], shared, False, 0, *static, late, zeros, slabs, parts[3:], acc)
    if shared:
        back = send(right, pairs(lambda y, x, z, c: (y + 2, x, z, c) if y % 2 != here else None))
        right = jnp.where(plane == here, right, back)
    return jnp.concatenate([left, right], axis=1)


def per_device(slab, slab_mask, order, integrals, integral_mask, row_owner):
    row, col = lax.axis_index("row"), lax.axis_index("col")
    core = row % 2
    zero = jnp.sum(jnp.arange(4, dtype=jnp.int32) * (1 - slab_mask[:, 0]))
    tiles = slab.reshape(4, TW, TW)
    kept = jnp.where(jnp.arange(3, dtype=jnp.int32)[:, None, None] >= zero, tiles[1:], tiles[:3])
    payload = jnp.concatenate(
        [kept.reshape(3 * TW, TW), jnp.full((PAD, TW), zero.astype(jnp.float32), jnp.float32).astype(jnp.bfloat16)], axis=0
    )

    high, x, z = col // (SIDE * SIDE), (col // SIDE) % SIDE, col % SIDE
    high_q, x_q, z_q = order // (SIDE * SIDE), (order // SIDE) % SIDE, order % SIDE
    sign = jnp.where(core == 0, 1, -1)
    dx, dz = (sign * (x - x_q)) % SIDE, (sign * (z - z_q)) % SIDE
    own = high_q == high
    arr = jnp.where(own, dz, 4 + dx).astype(jnp.int32)
    slot = jnp.where(own, dx, dz).astype(jnp.int32)

    masks = integral_mask.reshape(-1)
    planes = row_owner // 2
    branches = [functools.partial(run, (a, b)) for a in range(2) for b in range(2)]
    return lax.switch(planes[0] * 2 + planes[1], branches, payload, arr, slot, integrals, masks, row_owner)


def solution(mesh):
    return jax.shard_map(
        per_device,
        mesh=mesh,
        in_specs=(
            P("row", "col"),
            P("row", "col"),
            P(),
            P(None, "row", "col"),
            P(None, "row", "col"),
            P(),
        ),
        out_specs=P("row", "col"),
        check_vma=False,
    )
```
